32 devices in a mesh: seq: 8 (over z, x), head: 4 (over y, core).
Axes of the slice: x: 2, y: 2, z: 4, core: 2. Of those that a mesh axis runs over, the one named last changes fastest.
Arguments:
- tokens: bfloat16 [2048, 1024], P('seq'), may hold values from -6 to 6
- queries: bfloat16 [2048, 1024], P('seq', 'head'), may hold values from -8 to 8
- key_rows: bfloat16 [2048, 1024], P('seq', 'head'), may hold values from -8 to 8
- values: bfloat16 [2048, 1024], P('seq', 'head'), may hold values from -6 to 6
- ssm_input: bfloat16 [2048, 2048], P('seq', 'head'), may hold values from -6 to 6
- write_proj: bfloat16 [2048, 128], P('seq'), may hold values from -6 to 6
- read_proj: bfloat16 [2048, 128], P('seq'), may hold values from -6 to 6
- log_decay: float32 [32, 2048], P('head', 'seq'), may hold values from -1 to 0
- attn_project: bfloat16 [1024, 1024], P('head'), may hold values from -0.1875 to 0.1875
- ssm_project: bfloat16 [2048, 1024], P('head'), may hold values from -0.125 to 0.125
- gauss_project: bfloat16 [1024, 768], replicated, may hold values from -0.1875 to 0.1875
- tile_owner: int32 [2048], P('seq'), may hold values from 0 to 3, as said below
Outputs:
- block_out: bfloat16 [2048, 1024], P(('seq', 'head'))
- tile_rows: bfloat16 [8, 4, 4, 32, 768], P('seq', 'head')
The draws below stay inside these ranges and needn't reach their ends.
Inputs may be any that keep to these rules, and one draw needn't show every extreme that they name: `tile_owner`: in each aligned group of 64 tokens no owner is named by more than 32 tokens; in every block of 256 tokens one owner is named by exactly 32 tokens of each of its groups.
All inputs are finite; a program needn't handle non-finite values.
Results may differ from the reference program's by a relative error of at most 0.023.
Values may be sent and summed in bfloat16 or wider, within the bound.
A program may use at most 128 MiB of HBM per device.

```python
import math
import jax
import jax.numpy as jnp
from jax import lax

D = 1024
HEADS = 16
HDIM = 64
STATE_SPACE_HEADS = 32
SSM_HDIM = 64
STATE = 128
GW = 768
TOK_DEV = 256
SEQUENCE_TOKENS = 2048
BLOCKS = 8
OWNERS = 4
SUB = 64
CAP = 32


def query_key_pair(key):
    width_all = HEADS * HDIM
    base_key = jax.random.fold_in(key, 71)
    key_query = jax.random.fold_in(base_key, 0)
    key_keys = jax.random.fold_in(base_key, 1)
    key_faint = jax.random.fold_in(base_key, 4)
    query_drawn = jnp.clip(1.5 * jax.random.normal(key_query, (SEQUENCE_TOKENS, width_all), jnp.float32), -8.0, 8.0)
    keys_drawn = jnp.clip(1.5 * jax.random.normal(key_keys, (SEQUENCE_TOKENS, width_all), jnp.float32), -8.0, 8.0)
    row_index = jnp.arange(SEQUENCE_TOKENS, dtype=jnp.int32)[:, None]
    column_index = jnp.arange(width_all, dtype=jnp.int32)[None, :]
    within_head = column_index % HDIM
    quiet_count = max(1, HDIM // 4)
    is_quiet = within_head >= HDIM - quiet_count
    half_rows = SEQUENCE_TOKENS // 2
    faint_signs = jnp.where(jax.random.bernoulli(key_faint, 0.5, (SEQUENCE_TOKENS, width_all)), 1.0, -1.0)
    faint_level = 20.0 / math.sqrt(HDIM)
    faint_query = jnp.where(is_quiet, 8.0 * faint_signs, 0.0)
    faint_key = jnp.where(is_quiet, faint_level * faint_signs, 0.0)
    query_out = jnp.where(row_index % 64 == 21, faint_query, query_drawn)
    keys_out = jnp.where((row_index - half_rows) % 64 == 21, jnp.roll(faint_key, half_rows, axis=0), keys_drawn)
    return (query_out, keys_out)


def draw_queries(key, part):
    return query_key_pair(key)[0].astype(jnp.bfloat16)


def draw_key_rows(key, part):
    return query_key_pair(key)[1].astype(jnp.bfloat16)


def draw_log_decay(key, part):
    base_key = jax.random.fold_in(key, 33)
    key_kind, key_fast, key_slow, key_block, key_token, key_location, key_nesting_depth = jax.random.split(base_key, 7)
    fast_share = 0.5
    is_fast = jax.random.uniform(key_kind, (STATE_SPACE_HEADS, 1), jnp.float32) < fast_share
    fast_rate = jnp.exp(jax.random.uniform(key_fast, (STATE_SPACE_HEADS, 1), jnp.float32, math.log(1.0 / 50.0), math.log(1.0 / 30.0)))
    slow_rate = jnp.exp(jax.random.uniform(key_slow, (STATE_SPACE_HEADS, 1), jnp.float32, math.log(0.1 / SEQUENCE_TOKENS), math.log(0.4 / SEQUENCE_TOKENS)))
    head_frequency = jnp.where(is_fast, fast_rate, slow_rate)
    block_multiplier = jax.random.uniform(key_block, (STATE_SPACE_HEADS, SEQUENCE_TOKENS // TOK_DEV), jnp.float32, 0.6, 1.2)
    block_multiplier = jnp.repeat(block_multiplier, TOK_DEV, axis=1)
    token_multiplier = jax.random.uniform(key_token, (STATE_SPACE_HEADS, SEQUENCE_TOKENS), jnp.float32, 0.5, 1.5)
    flurry_location = jax.random.randint(key_location, (STATE_SPACE_HEADS, 2), 0, SEQUENCE_TOKENS)
    flurry_depth = jnp.log(jax.random.uniform(key_nesting_depth, (STATE_SPACE_HEADS, 2), jnp.float32, 0.5, 0.8))
    token_positions = jnp.arange(SEQUENCE_TOKENS, dtype=jnp.int32)[None, :]
    flurry_groups = jnp.where(token_positions == flurry_location[:, 0:1], flurry_depth[:, 0:1], 0.0)
    flurry_groups = flurry_groups + jnp.where(token_positions == flurry_location[:, 1:2], flurry_depth[:, 1:2], 0.0)
    return -head_frequency * block_multiplier * token_multiplier + flurry_groups


def draw_tile_owner(key, part):
    base_key = jax.random.fold_in(key, 57)
    key_star, key_other, key_order = jax.random.split(base_key, 3)
    group_count = SEQUENCE_TOKENS // SUB
    star = jax.random.randint(key_star, (SEQUENCE_TOKENS // TOK_DEV,), 0, OWNERS)
    star_group = jnp.repeat(star, TOK_DEV // SUB)
    others = (star_group[:, None] + jax.random.randint(key_other, (group_count, SUB), 1, OWNERS)) % OWNERS
    position = jnp.arange(SUB, dtype=jnp.int32)[None, :]
    listed = jnp.where(position < CAP, star_group[:, None], others)
    order_keys = jax.random.randint(key_order, (group_count, SUB), 0, 1048576) * SUB + position
    order = jnp.argsort(order_keys, axis=1, stable=True)
    shuffled = jnp.take_along_axis(listed, order, axis=1)
    return shuffled.reshape(SEQUENCE_TOKENS).astype(jnp.int32)


def levels(own_key, extent, shards, least, high):
    gain = 1.0
    for dim, blocks in shards:
        heights = jax.random.uniform(jax.random.fold_in(jax.random.fold_in(own_key, 6), dim), (blocks,), jnp.float32, least / len(shards), high / len(shards))
        gain = gain * jnp.repeat(jnp.exp(heights), extent[dim] // blocks).reshape((-1,) + (1,) * (len(extent) - 1 - dim))
    return gain


def noise(rng, dims, deviation, bound, cuts=(), held_as=jnp.bfloat16):
    values = jax.random.normal(rng, dims, jnp.float32) * deviation
    if len(cuts) > 0:
        values = levels(rng, dims, cuts, -0.22, 0.18) * values
    return jnp.clip(values, min=-bound, max=bound).astype(held_as)


def setup_inputs(seed: int = 0) -> dict:
    splits = jax.random.split(jax.random.key(seed), 13)
    return {
        "tokens": noise(splits[0], (SEQUENCE_TOKENS, D), 1.0, 6.0, ((0, 8),)),
        "queries": draw_queries(jax.random.fold_in(splits[12], 71), 0),
        "key_rows": draw_key_rows(jax.random.fold_in(splits[12], 71), 0),
        "values": noise(splits[3], (SEQUENCE_TOKENS, HEADS * HDIM), 1.0, 6.0, ((0, 8), (1, 4))),
        "ssm_input": noise(splits[4], (SEQUENCE_TOKENS, STATE_SPACE_HEADS * SSM_HDIM), 1.0, 6.0, ((0, 8), (1, 4))),
        "write_proj": noise(splits[5], (SEQUENCE_TOKENS, STATE), 1.0, 6.0, ((0, 8),)),
        "read_proj": noise(splits[6], (SEQUENCE_TOKENS, STATE), 1.0, 6.0, ((0, 8),)),
        "log_decay": draw_log_decay(jax.random.fold_in(splits[12], 71), 0),
        "attn_project": noise(splits[8], (HEADS * HDIM, D), (HEADS * HDIM) ** -0.5, 0.1875, ((0, 4),)),
        "ssm_project": noise(splits[9], (STATE_SPACE_HEADS * SSM_HDIM, D), (STATE_SPACE_HEADS * SSM_HDIM) ** -0.5, 0.125, ((0, 4),)),
        "gauss_project": noise(splits[10], (D, GW), D ** -0.5, 0.1875),
        "tile_owner": draw_tile_owner(jax.random.fold_in(splits[12], 71), 0),
    }


HIGHEST = lax.Precision.HIGHEST

def to_low(array):
    low = array.astype(jnp.bfloat16)
    low = lax.optimization_barrier(low)
    return low.astype(jnp.float32)

def attend_head(query_head, key_head, value_head):
    block_rows = math.gcd(SEQUENCE_TOKENS, 512)
    scale = 1.0 / math.sqrt(HDIM)

    def one_block(query_block):
        scores = jnp.dot(query_block, key_head.T, preferred_element_type=jnp.float32) * scale
        row_top = lax.optimization_barrier(jnp.max(scores, axis=1, keepdims=True))
        raised = jnp.exp(scores - row_top)
        totals = lax.optimization_barrier(jnp.sum(raised, axis=1, keepdims=True))
        weights = raised.astype(jnp.bfloat16)
        return jnp.dot(weights, value_head, preferred_element_type=jnp.float32) / totals
    blocks_in = query_head.reshape(SEQUENCE_TOKENS // block_rows, block_rows, HDIM)
    return lax.map(one_block, blocks_in).reshape(SEQUENCE_TOKENS, HDIM)

def chain_pieces(ssm_input, write_proj, read_proj, log_decay):
    row_count = write_proj.shape[0]
    head_count = log_decay.shape[0]
    head_width = ssm_input.shape[1] // head_count
    cumulative = jnp.cumsum(log_decay, axis=1)
    inputs_wide = ssm_input.astype(jnp.float32).reshape(row_count, head_count, head_width)
    later_rows = lax.broadcasted_iota(jnp.int32, (row_count, row_count), 0)
    earlier_cols = lax.broadcasted_iota(jnp.int32, (row_count, row_count), 1)
    log_gaps = cumulative[:, :, None] - cumulative[:, None, :]
    decays = jnp.exp(jnp.where((later_rows >= earlier_cols)[None], log_gaps, -jnp.inf))
    cross_terms = jnp.dot(read_proj, write_proj.T, preferred_element_type=jnp.float32)
    mixing = to_low(decays * cross_terms[None])
    inner_part = jnp.einsum('hts,shp->thp', mixing, inputs_wide, precision=HIGHEST)
    tail_decay = jnp.exp(cumulative[:, -1:] - cumulative)
    tail_inputs = to_low(inputs_wide * tail_decay.T[:, :, None])
    local_state = jnp.einsum('sn,shp->hnp', write_proj.astype(jnp.float32), tail_inputs, precision=HIGHEST)
    total_decay = jnp.exp(cumulative[:, -1])
    return (cumulative, inner_part, local_state, total_decay)

def chain_output(cumulative, inner_part, entering, read_proj):
    entering_low = to_low(entering)
    outer_part = jnp.einsum('tn,hnp->thp', read_proj.astype(jnp.float32), entering_low, precision=HIGHEST)
    mixture = inner_part + outer_part * jnp.exp(cumulative).T[:, :, None]
    scaled = mixture * lax.rsqrt(lax.optimization_barrier(jnp.mean(mixture * mixture, axis=2, keepdims=True)) + 1e-05)
    return scaled.reshape(scaled.shape[0], -1).astype(jnp.bfloat16)

def reference(tokens, queries, key_rows, values, ssm_input, write_proj, read_proj, log_decay, attn_project, ssm_project, gauss_project, tile_owner):
    query_all = queries.reshape(SEQUENCE_TOKENS, HEADS, HDIM).transpose(1, 0, 2)
    key_all = key_rows.reshape(SEQUENCE_TOKENS, HEADS, HDIM).transpose(1, 0, 2)
    value_all = values.reshape(SEQUENCE_TOKENS, HEADS, HDIM).transpose(1, 0, 2)
    heads_out = lax.map(lambda group: attend_head(group[0], group[1], group[2]), (query_all, key_all, value_all))
    attended = heads_out.transpose(1, 0, 2).reshape(SEQUENCE_TOKENS, HEADS * HDIM).astype(jnp.bfloat16)
    block_count = SEQUENCE_TOKENS // TOK_DEV
    input_blocks = ssm_input.reshape(block_count, TOK_DEV, STATE_SPACE_HEADS * SSM_HDIM)
    write_blocks = write_proj.reshape(block_count, TOK_DEV, STATE)
    read_blocks = read_proj.reshape(block_count, TOK_DEV, STATE)
    decay_blocks = log_decay.reshape(STATE_SPACE_HEADS, block_count, TOK_DEV).transpose(1, 0, 2)

    def advance(entering, block_parts):
        input_block, write_block, read_block, decay_block = block_parts
        cumulative, inner_part, local_state, total_decay = chain_pieces(input_block, write_block, read_block, decay_block)
        mixed_rows = chain_output(cumulative, inner_part, entering, read_block)
        leaving = total_decay[:, None, None] * entering + local_state
        return (leaving, mixed_rows)
    start_state = jnp.zeros((STATE_SPACE_HEADS, STATE, SSM_HDIM), jnp.float32)
    final_state, mixed_all = lax.scan(advance, start_state, (input_blocks, write_blocks, read_blocks, decay_blocks))
    ssm_mix = mixed_all.reshape(SEQUENCE_TOKENS, STATE_SPACE_HEADS * SSM_HDIM)
    update = jnp.dot(attended, attn_project, preferred_element_type=jnp.float32) + jnp.dot(ssm_mix, ssm_project, preferred_element_type=jnp.float32)
    block_out = (tokens.astype(jnp.float32) + update).astype(jnp.bfloat16)
    gauss = jnp.dot(block_out, gauss_project, preferred_element_type=jnp.float32).astype(jnp.bfloat16)
    one_hot = (tile_owner[:, None] == jnp.arange(OWNERS, dtype=jnp.int32)[None, :]).astype(jnp.int32)
    grouped = one_hot.reshape(SEQUENCE_TOKENS // SUB, SUB, OWNERS)
    slot_rank = lax.optimization_barrier(jnp.sum((jnp.cumsum(grouped, axis=1) - grouped) * grouped, axis=2)).reshape(SEQUENCE_TOKENS).astype(jnp.int32)
    token_positions = jnp.arange(SEQUENCE_TOKENS, dtype=jnp.int32)
    block_index = token_positions // TOK_DEV
    group_index = token_positions % TOK_DEV // SUB
    tile_rows = jnp.zeros((BLOCKS, OWNERS, OWNERS, CAP, GW), jnp.bfloat16)
    tile_rows = tile_rows.at[block_index, tile_owner, group_index, slot_rank].set(gauss)
    return (block_out, tile_rows)
```

```python
import functools
import math

import jax
import jax.numpy as jnp
from jax import lax
from jax.experimental import pallas as pl
from jax.experimental.pallas import tpu as pltpu
from jax.sharding import PartitionSpec as P

HDIM = 64
F32 = jnp.float32
BF16 = jnp.bfloat16
MESH = pl.DeviceIdType.MESH


def partner(index, step):
    out = index
    bit = 1
    while bit <= step:
        if step & bit:
            out = out + bit - 2 * bit * ((index // bit) % 2)
        bit *= 2
    return out


def dot(a, b):
    return jnp.dot(a, b, preferred_element_type=F32)


def dot_nt(a, b):
    return lax.dot_general(a, b, (((1,), (1,)), ((), ())), preferred_element_type=F32)


def dot_tn(a, b):
    return lax.dot_general(a, b, (((0,), (0,)), ((), ())), preferred_element_type=F32)


def kernel(
    seq,
    owners,
    tokens_hbm,
    queries_hbm,
    keys_hbm,
    values_hbm,
    ssm_hbm,
    write_hbm,
    read_hbm,
    decay_hbm,
    attn_w_hbm,
    ssm_w_hbm,
    gauss_w_hbm,
    owner_ref,
    block_out,
    tiles_out,
    tokens_v,
    queries_v,
    keys_v,
    values_v,
    ssm_v,
    write_v,
    read_v,
    decay_v,
    attn_w,
    ssm_w,
    gauss_w,
    kv_out,
    q_out,
    kv_in,
    q_in,
    st_out,
    st_in,
    en_out,
    en_in,
    acc,
    top,
    o_out,
    mix,
    inner,
    upd,
    up_out,
    up_in,
    pk_out,
    load_sem,
    kv_ss,
    kv_rs,
    q_ss,
    q_rs,
    fw_ss,
    fw_rs,
    st_ss,
    st_rs,
    en_ss,
    en_rs,
    o_ss,
    o_rs,
    up_ss,
    up_rs,
    tl_ss,
    tl_rs,
):
    me = lax.axis_index("seq")
    own = lax.axis_index("head")
    rows = queries_v.shape[0]
    heads = queries_v.shape[1] // HDIM
    members = seq // heads
    my_head = me // members
    my_group = me % members
    ssm_heads = decay_v.shape[0]
    width = ssm_v.shape[1] // ssm_heads
    part = st_in.shape[1] - 16
    sub = rows // owners
    cap = sub // 2

    def remote(src, dst, send, recv, target):
        return pltpu.make_async_remote_copy(
            src_ref=src, dst_ref=dst, send_sem=send, recv_sem=recv,
            device_id=target, device_id_type=MESH,
        )

    sources = [
        (queries_hbm, queries_v),
        (keys_hbm, keys_v),
        (values_hbm, values_v),
        (decay_hbm, decay_v),
        (ssm_hbm, ssm_v),
        (write_hbm, write_v),
        (read_hbm, read_v),
        (ssm_w_hbm, ssm_w),
        (attn_w_hbm, attn_w),
        (tokens_hbm.at[pl.ds(own * sub, sub)], tokens_v),
        (gauss_w_hbm, gauss_w),
    ]
    loads = [pltpu.make_async_copy(a, b, load_sem.at[i]) for i, (a, b) in enumerate(sources)]
    for load in loads:
        load.start()

    barrier = pltpu.get_barrier_semaphore()
    for r in range(1, seq):
        pl.semaphore_signal(barrier, inc=1, device_id={"seq": (me + r) % seq}, device_id_type=MESH)
    for r in range(1, owners):
        pl.semaphore_signal(
            barrier, inc=1, device_id={"head": (own + r) % owners}, device_id_type=MESH
        )

    loads[0].wait()
    q_t = (queries_v[...].astype(F32) * (1.0 / math.sqrt(HDIM))).astype(BF16).T
    for h in range(heads):
        q_out[h] = q_t[h * HDIM : (h + 1) * HDIM]
    loads[1].wait()
    loads[2].wait()
    for h in range(heads):
        cols = slice(h * HDIM, (h + 1) * HDIM)
        kv_out[h] = jnp.concatenate([keys_v[:, cols], values_v[:, cols]], axis=1)
    pl.semaphore_wait(barrier, seq - 1 + owners - 1)

    q_copies, kv_copies = [], []
    for r in range(1, heads):
        j = partner(my_head, r)
        target = {"seq": j * members + my_group}
        q_copies.append(remote(q_out.at[j], q_in.at[my_head], q_ss.at[r], q_rs.at[r], target))
        kv_copies.append(remote(kv_out.at[j], kv_in.at[me], kv_ss.at[r], kv_rs.at[r], target))

    def forward(r):
        slot = partner(my_head, r) * members + my_group
        source = kv_in.at[slot] if r else kv_out.at[my_head]
        copies = []
        for m in range(1, members):
            target = {"seq": my_head * members + (my_group + m) % members}
            copies.append(
                remote(source, kv_in.at[slot], fw_ss.at[r, m], fw_rs.at[r, m], target)
            )
        for copy in copies:
            copy.start()
        return copies

    for copy in q_copies:
        copy.start()
    forwards = {0: forward(0)}
    for copy in kv_copies:
        copy.start()
    q_in[my_head] = q_out[my_head]
    kv_in[me] = kv_out[my_head]

    loads[3].wait()
    log_decay = decay_v[...]
    high = log_decay.astype(BF16)
    rest = log_decay - high.astype(F32)
    middle = rest.astype(BF16)
    low = (rest - middle.astype(F32)).astype(BF16)
    s_index = lax.broadcasted_iota(jnp.int32, (rows, rows), 0)
    t_index = lax.broadcasted_iota(jnp.int32, (rows, rows), 1)
    causal = s_index <= t_index
    upto = jnp.where(causal, 1.0, 0.0).astype(BF16)
    cumulative = dot(high, upto) + dot(middle, upto) + dot(low, upto)
    block_end = cumulative[:, rows - 1 : rows]
    total = jnp.exp(block_end)
    loads[4].wait()
    loads[5].wait()
    ssm_t = ssm_v[...].T
    tail_decay = jnp.exp(block_end - cumulative)
    tails = jnp.concatenate(
        [
            (ssm_t[g * width : (g + 1) * width].astype(F32) * tail_decay[g : g + 1]).astype(BF16)
            for g in range(ssm_heads)
        ],
        axis=0,
    )
    local = dot(tails, write_v[...])
    for d in range(seq):
        g = d * part // width
        decay_rows = jnp.broadcast_to(total[g : g + 1], (8, local.shape[1]))
        decay_rest = decay_rows - decay_rows.astype(BF16).astype(F32)
        st_out[d] = jnp.concatenate(
            [local[d * part : (d + 1) * part], decay_rows, decay_rest], axis=0
        ).astype(BF16)
    st_copies = []
    for r in range(1, seq):
        d = (me + r) % seq
        st_copies.append(
            remote(st_out.at[d], st_in.at[me], st_ss.at[r], st_rs.at[r], {"seq": d})
        )
    for copy in st_copies:
        copy.start()
    st_in[me] = st_out[me]

    loads[6].wait()
    cross = dot_nt(write_v[...], read_v[...])
    cum_cols = jnp.concatenate(
        [cumulative, jnp.zeros((128 - ssm_heads, rows), F32)], axis=0
    ).T
    for g in range(ssm_heads):
        gaps = cumulative[g : g + 1] - cum_cols[:, g : g + 1]
        mixing = (jnp.exp(jnp.where(causal, gaps, -jnp.inf)) * cross).astype(BF16)
        inner[g * width : (g + 1) * width] = dot(ssm_t[g * width : (g + 1) * width], mixing)

    for r in range(1, heads):
        kv_copies[r - 1].wait_recv()
        forwards[r] = forward(r)

    for copy in st_copies:
        copy.wait_recv()
    state = jnp.zeros((part, local.shape[1]), F32)
    for b in range(seq):
        en_out[b] = state.astype(BF16)
        if b < seq - 1:
            arrived = st_in[b].astype(F32)
            decay = arrived[part : part + 1] + arrived[part + 8 : part + 9]
            state = decay * state + arrived[:part]
    en_copies = []
    for r in range(1, seq):
        d = (me + r) % seq
        en_copies.append(
            remote(en_out.at[d], en_in.at[me], en_ss.at[r], en_rs.at[r], {"seq": d})
        )
    for copy in en_copies:
        copy.start()
    en_in[me] = en_out[me]

    for copy in q_copies:
        copy.wait_recv()
    key_rows = members * rows
    below = lax.broadcasted_iota(jnp.int32, (2 * HDIM, key_rows), 0) < HDIM
    zeros = jnp.zeros((HDIM, rows), BF16)
    for r in range(heads):
        for m in range(1, members):
            forwards[r][m - 1].wait_recv()
        a = partner(my_head, r)
        kv = kv_in[pl.ds(a * members, members)].reshape(key_rows, 2 * HDIM)
        v_t = jnp.where(below, jnp.ones((), BF16), kv.T)
        for c in range(heads):
            scores = dot(kv, jnp.concatenate([q_in[c], zeros], axis=0))
            highest = jnp.max(scores, axis=0, keepdims=True)
            if r:
                before = top[c, 0:1]
                highest = jnp.maximum(highest, before)
            weights = jnp.exp(scores - highest).astype(BF16)
            summed = dot(v_t, weights)
            if r:
                summed = summed + acc[c] * jnp.exp(before - highest)
            if r < heads - 1:
                acc[c] = summed
                top[c] = jnp.broadcast_to(highest, (8, rows))
            else:
                o_out[c] = (summed[HDIM:] / summed[0:1]).astype(BF16)
    o_copies = []
    for r in range(1, heads):
        j = partner(my_head, r)
        o_copies.append(
            remote(
                o_out.at[j], mix.at[my_head], o_ss.at[r], o_rs.at[r],
                {"seq": j * members + my_group},
            )
        )
    for copy in o_copies:
        copy.start()
    mix[my_head] = o_out[my_head]

    for copy in en_copies:
        copy.wait_recv()
    entering = en_in[...]
    if part % 16:
        entering = entering.astype(F32)
    entering = entering.reshape(seq * part, local.shape[1]).astype(BF16)
    outer = dot_nt(entering, read_v[...])
    grown = jnp.exp(cumulative)
    mixed = []
    for g in range(ssm_heads):
        span = slice(g * width, (g + 1) * width)
        out = inner[span] + outer[span] * grown[g : g + 1]
        mean = jnp.mean(out * out, axis=0, keepdims=True)
        mixed.append((out * lax.rsqrt(mean + 1e-05)).astype(BF16))
    loads[7].wait()
    upd[...] = dot_tn(jnp.concatenate(mixed, axis=0), ssm_w[...])

    named = jnp.zeros((1, sub), jnp.int32)
    for q in range(owners):
        named = jnp.where(own == q, owner_ref[:, q * sub : (q + 1) * sub], named)
    one_hot = jnp.where(
        lax.broadcasted_iota(jnp.int32, (8, sub), 0) == named, 1.0, 0.0
    )
    earlier = jnp.where(
        lax.broadcasted_iota(jnp.int32, (sub, sub), 0)
        < lax.broadcasted_iota(jnp.int32, (sub, sub), 1),
        1.0,
        0.0,
    )
    counted = dot(one_hot.astype(BF16), earlier.astype(BF16))
    rank = jnp.sum(counted * one_hot, axis=0, keepdims=True)
    slot = named * cap + rank.astype(jnp.int32)
    selector = jnp.where(
        lax.broadcasted_iota(jnp.int32, (owners * cap, sub), 0) == slot, 1.0, 0.0
    ).astype(BF16)

    loads[8].wait()
    for copy in o_copies:
        copy.wait_recv()
    attended = mix[...].reshape(heads * HDIM, rows)
    update = upd[...] + dot_tn(attended, attn_w[...])
    for q in range(owners):
        up_out[q] = update[q * sub : (q + 1) * sub].astype(BF16)
    up_copies = []
    for r in (3, 2, 1) if owners == 4 else range(1, owners):
        q = partner(own, r)
        up_copies.append(
            remote(up_out.at[q], up_in.at[r], up_ss.at[r], up_rs.at[r], {"head": q})
        )
    for copy in up_copies:
        copy.start()
    loads[9].wait()
    loads[10].wait()
    summed = up_out[own].astype(F32)
    for copy in up_copies:
        copy.wait_recv()
    for r in range(1, owners):
        summed = summed + up_in[r].astype(F32)
    block = (tokens_v[...].astype(F32) + summed).astype(BF16)
    block_out[...] = block
    gauss = dot(block, gauss_w[...]).astype(BF16)
    packed = dot(selector, gauss).astype(BF16)
    for q in range(owners):
        pk_out[q] = packed[q * cap : (q + 1) * cap]
    tl_copies = []
    for r in (3, 2, 1) if owners == 4 else range(1, owners):
        q = partner(own, r)
        tl_copies.append(
            remote(pk_out.at[q], tiles_out.at[0, 0, own], tl_ss.at[r], tl_rs.at[r], {"head": q})
        )
    for copy in tl_copies:
        copy.start()
    tiles_out[0, 0, own] = pk_out[own]
    for copy in q_copies + kv_copies + st_copies + en_copies + o_copies + up_copies:
        copy.wait_send()
    for copies in forwards.values():
        for copy in copies:
            copy.wait_send()
    for copy in tl_copies:
        copy.wait()


def per_device(seq, owners, *args):
    (tokens, queries, key_rows, values, ssm_input, write_proj, read_proj, log_decay,
     attn_project, ssm_project, gauss_project, tile_owner) = args
    rows = queries.shape[0]
    heads = queries.shape[1] // HDIM
    members = seq // heads
    model = tokens.shape[1]
    sub = rows // owners
    cap = sub // 2
    gauss_width = gauss_project.shape[1]
    channels = ssm_input.shape[1]
    state = write_proj.shape[1]
    part = channels // seq
    hbm = pl.BlockSpec(memory_space=pl.ANY)
    vmem = pl.BlockSpec(memory_space=pltpu.VMEM)
    dma = pltpu.SemaphoreType.DMA
    like = lambda a: pltpu.VMEM(a.shape, a.dtype)
    return pl.pallas_call(
        functools.partial(kernel, seq, owners),
        out_shape=(
            jax.ShapeDtypeStruct((sub, model), BF16),
            jax.ShapeDtypeStruct((1, 1, owners, cap, gauss_width), BF16),
        ),
        in_specs=[hbm] * 11 + [vmem],
        out_specs=(vmem, vmem),
        scratch_shapes=[
            pltpu.VMEM((sub, model), BF16),
            like(queries),
            like(key_rows),
            like(values),
            like(ssm_input),
            like(write_proj),
            like(read_proj),
            like(log_decay),
            like(attn_project),
            like(ssm_project),
            like(gauss_project),
            pltpu.VMEM((heads, rows, 2 * HDIM), BF16),
            pltpu.VMEM((heads, HDIM, rows), BF16),
            pltpu.VMEM((seq, rows, 2 * HDIM), BF16),
            pltpu.VMEM((heads, HDIM, rows), BF16),
            pltpu.VMEM((seq, part + 16, state), BF16),
            pltpu.VMEM((seq, part + 16, state), BF16),
            pltpu.VMEM((seq, part, state), BF16),
            pltpu.VMEM((seq, part, state), BF16),
            pltpu.VMEM((heads, 2 * HDIM, rows), F32),
            pltpu.VMEM((heads, 8, rows), F32),
            pltpu.VMEM((heads, HDIM, rows), BF16),
            pltpu.VMEM((heads, HDIM, rows), BF16),
            pltpu.VMEM((channels, rows), F32),
            pltpu.VMEM((rows, model), F32),
            pltpu.VMEM((owners, sub, model), BF16),
            pltpu.VMEM((owners, sub, model), BF16),
            pltpu.VMEM((owners, cap, gauss_width), BF16),
            dma((11,)),
            dma((heads,)),
            dma((heads,)),
            dma((heads,)),
            dma((heads,)),
            dma((heads, members)),
            dma((heads, members)),
            dma((seq,)),
            dma((seq,)),
            dma((seq,)),
            dma((seq,)),
            dma((heads,)),
            dma((heads,)),
            dma((owners,)),
            dma((owners,)),
            dma((owners,)),
            dma((owners,)),
        ],
        compiler_params=pltpu.CompilerParams(
            collective_id=0, has_side_effects=True, vmem_limit_bytes=56 * 1024 * 1024
        ),
    )(tokens, queries, key_rows, values, ssm_input, write_proj, read_proj, log_decay,
      attn_project, ssm_project, gauss_project, tile_owner.reshape(1, rows))


def solution(mesh):
    in_specs = (
        P("seq", None),
        P("seq", "head"),
        P("seq", "head"),
        P("seq", "head"),
        P("seq", "head"),
        P("seq", None),
        P("seq", None),
        P("head", "seq"),
        P("head", None),
        P("head", None),
        P(),
        P("seq"),
    )
    out_specs = (P(("seq", "head"), None), P("seq", "head", None, None, None))
    return jax.shard_map(
        functools.partial(per_device, mesh.shape["seq"], mesh.shape["head"]),
        mesh=mesh,
        in_specs=in_specs,
        out_specs=out_specs,
        check_vma=False,
    )
```

```python
import functools
import math

import jax
import jax.numpy as jnp
from jax import lax
from jax.experimental import pallas as pl
from jax.experimental.pallas import tpu as pltpu
from jax.sharding import PartitionSpec as P

HDIM = 64
F32 = jnp.float32
BF16 = jnp.bfloat16
MESH = pl.DeviceIdType.MESH


def partner(index, step):
    out = index
    bit = 1
    while bit <= step:
        if step & bit:
            out = out + bit - 2 * bit * ((index // bit) % 2)
        bit *= 2
    return out


def dot(a, b):
    return jnp.dot(a, b, preferred_element_type=F32)


def dot_nt(a, b):
    return lax.dot_general(a, b, (((1,), (1,)), ((), ())), preferred_element_type=F32)


def dot_tn(a, b):
    return lax.dot_general(a, b, (((0,), (0,)), ((), ())), preferred_element_type=F32)


def kernel(
    seq,
    owners,
    tokens_hbm,
    queries_hbm,
    keys_hbm,
    values_hbm,
    ssm_hbm,
    write_hbm,
    read_hbm,
    decay_hbm,
    attn_w_hbm,
    ssm_w_hbm,
    gauss_w_hbm,
    owner_ref,
    block_out,
    tiles_out,
    tokens_v,
    queries_v,
    keys_v,
    values_v,
    ssm_v,
    write_v,
    read_v,
    decay_v,
    attn_w,
    ssm_w,
    gauss_w,
    kv_out,
    q_out,
    kv_in,
    q_in,
    st_out,
    st_in,
    en_out,
    en_in,
    acc,
    top,
    o_out,
    o_in,
    inner,
    up_out,
    up_in,
    block_v,
    pk_out,
    load_sem,
    out_sem,
    wt_ss,
    wt_rs,
    kv_ss,
    kv_rs,
    q_ss,
    q_rs,
    fw_ss,
    fw_rs,
    st_ss,
    st_rs,
    en_ss,
    en_rs,
    o_ss,
    o_rs,
    up_ss,
    up_rs,
    tl_ss,
    tl_rs,
):
    me = lax.axis_index("seq")
    own = lax.axis_index("head")
    rows = queries_v.shape[0]
    heads = queries_v.shape[1] // HDIM
    members = seq // heads
    my_head = me // members
    my_group = me % members
    ssm_heads = decay_v.shape[0]
    width = ssm_v.shape[1] // ssm_heads
    part = st_in.shape[1] - 16
    sub = rows // owners
    cap = sub // 2

    started = []

    def remote(src, dst, send, recv, target):
        copy = pltpu.make_async_remote_copy(
            src_ref=src, dst_ref=dst, send_sem=send, recv_sem=recv,
            device_id=target, device_id_type=MESH,
        )
        started.append(copy)
        return copy

    sources = [
        (queries_hbm, queries_v),
        (keys_hbm, keys_v),
        (values_hbm, values_v),
        (decay_hbm, decay_v),
        (ssm_hbm, ssm_v),
        (write_hbm, write_v),
        (read_hbm, read_v),
        (ssm_w_hbm, ssm_w),
        (attn_w_hbm, attn_w.at[own]),
        (tokens_hbm.at[pl.ds(own * sub, sub)], tokens_v),
        (gauss_w_hbm, gauss_w),
    ]
    loads = [pltpu.make_async_copy(a, b, load_sem.at[i]) for i, (a, b) in enumerate(sources)]
    for load in loads:
        load.start()

    barrier = pltpu.get_barrier_semaphore()
    for r in range(1, seq):
        pl.semaphore_signal(barrier, inc=1, device_id={"seq": (me + r) % seq}, device_id_type=MESH)
    for r in range(1, owners):
        for step in range(heads):
            target = {
                "seq": partner(my_head, step) * members + my_group,
                "head": partner(own, r),
            }
            pl.semaphore_signal(barrier, inc=1, device_id=target, device_id_type=MESH)

    loads[0].wait()
    q_t = (queries_v[...].astype(F32) * (1.0 / math.sqrt(HDIM))).astype(BF16).T
    for h in range(heads):
        q_out[h] = q_t[h * HDIM : (h + 1) * HDIM]
    loads[1].wait()
    loads[2].wait()
    for h in range(heads):
        cols = slice(h * HDIM, (h + 1) * HDIM)
        kv_out[h] = jnp.concatenate([keys_v[:, cols], values_v[:, cols]], axis=1)
    pl.semaphore_wait(barrier, seq - 1 + (owners - 1) * heads)

    q_copies, kv_copies = [], []
    for r in range(1, heads):
        j = partner(my_head, r)
        target = {"seq": j * members + my_group}
        q_copies.append(remote(q_out.at[j], q_in.at[my_head], q_ss.at[r], q_rs.at[r], target))
        kv_copies.append(remote(kv_out.at[j], kv_in.at[me], kv_ss.at[r], kv_rs.at[r], target))

    def forward(r):
        slot = partner(my_head, r) * members + my_group
        source = kv_in.at[slot] if r else kv_out.at[my_head]
        copies = []
        for m in range(1, members):
            target = {"seq": my_head * members + (my_group + m) % members}
            copies.append(
                remote(source, kv_in.at[slot], fw_ss.at[r, m], fw_rs.at[r, m], target)
            )
        for copy in copies:
            copy.start()
        return copies

    for copy in q_copies:
        copy.start()
    forwards = {0: forward(0)}
    for copy in kv_copies:
        copy.start()
    loads[8].wait()
    far = partner(own, 2)
    wt_copies = [
        remote(attn_w.at[own], attn_w.at[own], wt_ss.at[r], wt_rs.at[r], {"head": partner(own, r)})
        for r in (2, 1)
    ]
    for copy in wt_copies:
        copy.start()
    q_in[my_head] = q_out[my_head]
    kv_in[me] = kv_out[my_head]

    loads[3].wait()
    log_decay = decay_v[...]
    high = log_decay.astype(BF16)
    rest = log_decay - high.astype(F32)
    middle = rest.astype(BF16)
    low = (rest - middle.astype(F32)).astype(BF16)
    s_index = lax.broadcasted_iota(jnp.int32, (rows, rows), 0)
    t_index = lax.broadcasted_iota(jnp.int32, (rows, rows), 1)
    causal = s_index <= t_index
    upto = jnp.where(causal, 1.0, 0.0).astype(BF16)
    cumulative = dot(high, upto) + dot(middle, upto) + dot(low, upto)
    block_end = cumulative[:, rows - 1 : rows]
    total = jnp.exp(block_end)
    loads[4].wait()
    loads[5].wait()
    ssm_t = ssm_v[...].T
    tail_decay = jnp.exp(block_end - cumulative)
    tails = jnp.concatenate(
        [
            (ssm_t[g * width : (g + 1) * width].astype(F32) * tail_decay[g : g + 1]).astype(BF16)
            for g in range(ssm_heads)
        ],
        axis=0,
    )
    local = dot(tails, write_v[...])
    for d in range(seq):
        g = d * part // width
        decay_rows = jnp.broadcast_to(total[g : g + 1], (8, local.shape[1]))
        decay_rest = decay_rows - decay_rows.astype(BF16).astype(F32)
        st_out[d] = jnp.concatenate(
            [local[d * part : (d + 1) * part], decay_rows, decay_rest], axis=0
        ).astype(BF16)
    st_copies = []
    for r in range(1, seq):
        d = (me + r) % seq
        st_copies.append(
            remote(st_out.at[d], st_in.at[me], st_ss.at[r], st_rs.at[r], {"seq": d})
        )
    for copy in st_copies:
        copy.start()
    st_in[me] = st_out[me]

    loads[6].wait()
    cross = dot_nt(write_v[...], read_v[...])
    cum_cols = jnp.concatenate(
        [cumulative, jnp.zeros((128 - ssm_heads, rows), F32)], axis=0
    ).T
    for g in range(ssm_heads):
        gaps = cumulative[g : g + 1] - cum_cols[:, g : g + 1]
        mixing = (jnp.exp(jnp.where(causal, gaps, -jnp.inf)) * cross).astype(BF16)
        inner[g * width : (g + 1) * width] = dot(ssm_t[g * width : (g + 1) * width], mixing)

    key_rows = members * rows
    below = lax.broadcasted_iota(jnp.int32, (2 * HDIM, key_rows), 0) < HDIM
    zeros = jnp.zeros((HDIM, rows), BF16)
    o_copies = []

    def attend(r):
        for m in range(1, members):
            forwards[r][m - 1].wait_recv()
        a = partner(my_head, r)
        kv = kv_in[pl.ds(a * members, members)].reshape(key_rows, 2 * HDIM)
        v_t = jnp.where(below, jnp.ones((), BF16), kv.T)
        for c in reversed(range(heads)):
            j = partner(my_head, c)
            scores = dot(kv, jnp.concatenate([q_in[j], zeros], axis=0))
            highest = jnp.max(scores, axis=0, keepdims=True)
            if r:
                before = top[c, 0:1]
                highest = jnp.maximum(highest, before)
            weights = jnp.exp(scores - highest).astype(BF16)
            summed = dot(v_t, weights)
            if r:
                summed = summed + acc[c] * jnp.exp(before - highest)
            if r < heads - 1:
                acc[c] = summed
                top[c] = jnp.broadcast_to(highest, (8, rows))
                continue
            head_out = summed[HDIM:] / summed[0:1]
            for q in range(owners):
                piece = head_out[:, q * sub : (q + 1) * sub]
                o_out[c, q] = jnp.concatenate(
                    [piece[: HDIM // 2], piece[HDIM // 2 :]], axis=1
                ).astype(BF16)
            slot = own * heads + my_head
            for step in reversed(range(owners)):
                q = partner(own, step)
                if c == 0 and step == 0:
                    o_in[slot] = o_out[c, q]
                    continue
                copy = remote(
                    o_out.at[c, q], o_in.at[slot], o_ss.at[c, step], o_rs.at[c, step],
                    {"seq": j * members + my_group, "head": q},
                )
                copy.start()
                o_copies.append(copy)

    def relay(r):
        kv_copies[r - 1].wait_recv()
        forwards[r] = forward(r)

    for copy in q_copies:
        copy.wait_recv()
    attend(0)
    relay(1)
    relay(2)
    attend(1)
    relay(3)

    for copy in st_copies:
        copy.wait_recv()
    state = jnp.zeros((part, local.shape[1]), F32)
    for b in range(seq):
        en_out[b] = state.astype(BF16)
        if b < seq - 1:
            arrived = st_in[b].astype(F32)
            decay = arrived[part : part + 1] + arrived[part + 8 : part + 9]
            state = decay * state + arrived[:part]
    en_copies = []
    for r in range(1, seq):
        d = (me + r) % seq
        en_copies.append(
            remote(en_out.at[d], en_in.at[me], en_ss.at[r], en_rs.at[r], {"seq": d})
        )
    for copy in en_copies:
        copy.start()
    en_in[me] = en_out[me]

    wt_copies[0].wait_recv()
    wt_relay = remote(
        attn_w.at[far], attn_w.at[far], wt_ss.at[3], wt_rs.at[3], {"head": partner(own, 1)}
    )
    wt_relay.start()
    attend(2)

    for copy in en_copies:
        copy.wait_recv()
    entering = en_in[...]
    if part % 16:
        entering = entering.astype(F32)
    entering = entering.reshape(seq * part, local.shape[1]).astype(BF16)
    outer = dot_nt(entering, read_v[...])
    grown = jnp.exp(cumulative)
    mixed = []
    for g in range(ssm_heads):
        span = slice(g * width, (g + 1) * width)
        out = inner[span] + outer[span] * grown[g : g + 1]
        mean = jnp.mean(out * out, axis=0, keepdims=True)
        mixed.append((out * lax.rsqrt(mean + 1e-05)).astype(BF16))
    loads[7].wait()
    update = dot_tn(jnp.concatenate(mixed, axis=0), ssm_w[...])
    for q in range(owners):
        up_out[q] = update[q * sub : (q + 1) * sub].astype(BF16)
    up_copies = []
    for r in (3, 2, 1):
        q = partner(own, r)
        up_copies.append(
            remote(up_out.at[q], up_in.at[r], up_ss.at[r], up_rs.at[r], {"head": q})
        )
    for copy in up_copies:
        copy.start()

    named = jnp.zeros((1, sub), jnp.int32)
    for q in range(owners):
        named = jnp.where(own == q, owner_ref[:, q * sub : (q + 1) * sub], named)
    one_hot = jnp.where(
        lax.broadcasted_iota(jnp.int32, (8, sub), 0) == named, 1.0, 0.0
    )
    earlier = jnp.where(
        lax.broadcasted_iota(jnp.int32, (sub, sub), 0)
        < lax.broadcasted_iota(jnp.int32, (sub, sub), 1),
        1.0,
        0.0,
    )
    counted = dot(one_hot.astype(BF16), earlier.astype(BF16))
    rank = jnp.sum(counted * one_hot, axis=0, keepdims=True)
    slot = named * cap + rank.astype(jnp.int32)
    selector = jnp.where(
        lax.broadcasted_iota(jnp.int32, (owners * cap, sub), 0) == slot, 1.0, 0.0
    ).astype(BF16)

    attend(3)
    loads[9].wait()
    loads[10].wait()
    summed = up_out[own].astype(F32)
    for copy in up_copies:
        copy.wait_recv()
    for r in range(1, owners):
        summed = summed + up_in[r].astype(F32)
    wt_copies[1].wait_recv()
    wt_relay.wait_recv()
    for copy in o_copies:
        copy.wait_recv()
    halves = o_in[...]
    attended = jnp.concatenate([halves[:, :, :sub], halves[:, :, sub:]], axis=1)
    attended = attended.reshape(owners * heads * HDIM, sub)
    summed = summed + dot_tn(attended, attn_w[...].reshape(owners * heads * HDIM, summed.shape[1]))
    block = (tokens_v[...].astype(F32) + summed).astype(BF16)
    block_v[...] = block
    block_copy = pltpu.make_async_copy(block_v, block_out, out_sem.at[0])
    block_copy.start()
    gauss = dot(block, gauss_w[...]).astype(BF16)
    packed = dot(selector, gauss).astype(BF16)
    for q in range(owners):
        pk_out[q] = packed[q * cap : (q + 1) * cap]
    tl_copies = []
    for r in (3, 2, 1):
        q = partner(own, r)
        tl_copies.append(
            remote(pk_out.at[q], tiles_out.at[0, 0, own], tl_ss.at[r], tl_rs.at[r], {"head": q})
        )
    for copy in tl_copies:
        copy.start()
    tile_copy = pltpu.make_async_copy(pk_out.at[own], tiles_out.at[0, 0, own], out_sem.at[1])
    tile_copy.start()
    for copy in tl_copies:
        copy.wait_recv()
    block_copy.wait()
    tile_copy.wait()
    for copy in started:
        copy.wait_send()


def hand_over(block_in, tiles_in, block_out, tiles_out, sem):
    copies = [
        pltpu.make_async_copy(block_in, block_out, sem.at[0]),
        pltpu.make_async_copy(tiles_in, tiles_out, sem.at[1]),
    ]
    for copy in copies:
        copy.start()
    for copy in copies:
        copy.wait()


def per_device(seq, owners, *args):
    (tokens, queries, key_rows, values, ssm_input, write_proj, read_proj, log_decay,
     attn_project, ssm_project, gauss_project, tile_owner) = args
    rows = queries.shape[0]
    heads = queries.shape[1] // HDIM
    members = seq // heads
    model = tokens.shape[1]
    sub = rows // owners
    cap = sub // 2
    gauss_width = gauss_project.shape[1]
    channels = ssm_input.shape[1]
    state = write_proj.shape[1]
    part = channels // seq
    hbm = pl.BlockSpec(memory_space=pl.ANY)
    vmem = pl.BlockSpec(memory_space=pltpu.VMEM)
    dma = pltpu.SemaphoreType.DMA
    like = lambda a: pltpu.VMEM(a.shape, a.dtype)
    shapes = (
        jax.ShapeDtypeStruct((sub, model), BF16),
        jax.ShapeDtypeStruct((1, 1, owners, cap, gauss_width), BF16),
    )
    results = pl.pallas_call(
        functools.partial(kernel, seq, owners),
        out_shape=shapes,
        in_specs=[hbm] * 11 + [vmem],
        out_specs=(hbm, hbm),
        scratch_shapes=[
            pltpu.VMEM((sub, model), BF16),
            like(queries),
            like(key_rows),
            like(values),
            like(ssm_input),
            like(write_proj),
            like(read_proj),
            like(log_decay),
            pltpu.VMEM((owners, *attn_project.shape), BF16),
            like(ssm_project),
            like(gauss_project),
            pltpu.VMEM((heads, rows, 2 * HDIM), BF16),
            pltpu.VMEM((heads, HDIM, rows), BF16),
            pltpu.VMEM((seq, rows, 2 * HDIM), BF16),
            pltpu.VMEM((heads, HDIM, rows), BF16),
            pltpu.VMEM((seq, part + 16, state), BF16),
            pltpu.VMEM((seq, part + 16, state), BF16),
            pltpu.VMEM((seq, part, state), BF16),
            pltpu.VMEM((seq, part, state), BF16),
            pltpu.VMEM((heads, 2 * HDIM, rows), F32),
            pltpu.VMEM((heads, 8, rows), F32),
            pltpu.VMEM((heads, owners, HDIM // 2, 2 * sub), BF16),
            pltpu.VMEM((owners * heads, HDIM // 2, 2 * sub), BF16),
            pltpu.VMEM((channels, rows), F32),
            pltpu.VMEM((owners, sub, model), BF16),
            pltpu.VMEM((owners, sub, model), BF16),
            pltpu.VMEM((sub, model), BF16),
            pltpu.VMEM((owners, cap, gauss_width), BF16),
            dma((11,)),
            dma((2,)),
            dma((owners,)),
            dma((owners,)),
            dma((heads,)),
            dma((heads,)),
            dma((heads,)),
            dma((heads,)),
            dma((heads, members)),
            dma((heads, members)),
            dma((seq,)),
            dma((seq,)),
            dma((seq,)),
            dma((seq,)),
            dma((heads, owners)),
            dma((heads, owners)),
            dma((owners,)),
            dma((owners,)),
            dma((owners,)),
            dma((owners,)),
        ],
        compiler_params=pltpu.CompilerParams(
            collective_id=0, has_side_effects=True, vmem_limit_bytes=56 * 1024 * 1024
        ),
    )(tokens, queries, key_rows, values, ssm_input, write_proj, read_proj, log_decay,
      attn_project, ssm_project, gauss_project, tile_owner.reshape(1, rows))
    return pl.pallas_call(
        hand_over,
        out_shape=shapes,
        in_specs=[hbm, hbm],
        out_specs=(hbm, hbm),
        scratch_shapes=[dma((2,))],
    )(*results)


def solution(mesh):
    in_specs = (
        P("seq", None),
        P("seq", "head"),
        P("seq", "head"),
        P("seq", "head"),
        P("seq", "head"),
        P("seq", None),
        P("seq", None),
        P("head", "seq"),
        P("head", None),
        P("head", None),
        P(),
        P("seq"),
    )
    out_specs = (P(("seq", "head"), None), P("seq", "head", None, None, None))
    return jax.shard_map(
        functools.partial(per_device, mesh.shape["seq"], mesh.shape["head"]),
        mesh=mesh,
        in_specs=in_specs,
        out_specs=out_specs,
        check_vma=False,
    )
```
